32 devices in a mesh: groups: 2 (over y), state: 4 (over z), member: 4 (over x, core).
Axes of the slice: x: 2, y: 2, z: 4, core: 2. Of those that a mesh axis runs over, the one named last changes fastest.
Arguments:
- ensemble: bfloat16 [256, 65536], P('member', ('groups', 'state')), parts along dimension 1, may hold values from -6 to 6
- obs_value: float32 [6, 1024], P(None, ('groups', 'state', 'member')), parts along dimension 1, may hold values from -6 to 6
- obs_var: float32 [6, 1024], P(None, ('groups', 'state', 'member')), parts along dimension 1, may hold values from 0.3 to 4
- obs_site: int32 [6, 1024], P(None, ('groups', 'state', 'member')), parts along dimension 1, may hold values from 0 to 2047
- loc_pattern: int32 [6, 32, 8], P(None, ('groups', 'state', 'member')), parts along dimension 1, may hold values 0 or 1
Outputs:
- posterior: bfloat16 [256, 65536], P('member', ('groups', 'state')), parts along dimension 1
The draws below stay inside these ranges and needn't reach their ends.
There are 2 independent parts, one for each index of `groups`. The reference program is written for one: setup_inputs(seed, part) draws one part's arguments, and reference() takes and returns one part's arrays. A program takes and returns all parts, laid end to end along the dimension named above; each array names one. Nothing has to cross between parts.
All inputs are finite; a program needn't handle non-finite values. No bound on the sum of `loc_pattern` on one device may be relied on, other than what follows from the above.
Results may differ from the reference program's by a relative error of at most 0.023.
Values may be sent and summed in bfloat16 or wider, within the bound.
A program may use at most 64 MiB of HBM per device.

```python
import math
import jax
import jax.numpy as jnp
from jax import lax

M = 256
NOBS = 512
OBS_TILE = 64
BATCHES = 6
S_DEV = 2048
NBLK = 16
OBS_DEV = 32
NTILE = 8
NS = 32768
N_STATE = 4
N_MEMBER = 4


def place_ends(values, key, low, top_value):
    longest = values.shape.index(max(values.shape))
    spots = []
    for shift in (0, 1):
        where = [jax.random.randint(jax.random.fold_in(key, axis), (), 0, length) for axis, length in enumerate(values.shape)]
        where[longest] = (where[longest] + shift) % values.shape[longest]
        spots.append(tuple(where))
    return values.at[spots[0]].set(low).at[spots[1]].set(top_value)


def block_scale(stream_key, dims, shards, low, largest):
    factor_of, own = 1.0, jax.random.fold_in(stream_key, 6)
    for axis_at, parts in shards:
        steps = jnp.exp(jax.random.uniform(jax.random.fold_in(own, axis_at), (parts,), jnp.float32, low / len(shards), largest / len(shards)))
        factor_of = factor_of * jnp.repeat(steps, dims[axis_at] // parts).reshape([-1 if axis == axis_at else 1 for axis in range(len(dims))])
    return factor_of


def normal_values(own_key, shape, width, reach, split=(), kind=jnp.bfloat16):
    values = width * jax.random.normal(own_key, shape, jnp.float32)
    if split:
        values = values * block_scale(own_key, shape, split, -0.22, 0.18)
    return jnp.clip(values, -reach, reach).astype(kind)


def setup_inputs(seed: int = 0, part: int = 0) -> dict:
    keys = jax.random.split(jax.random.key(seed), 6)
    part_keys = jax.random.split(jax.random.fold_in(keys[5], part), 6)
    return {
        "ensemble": normal_values(part_keys[0], (M, NS), 1.0, 6.0, ((0, 4), (1, 4))),
        "obs_value": normal_values(part_keys[1], (BATCHES, NOBS), 1.5, 6.0, ((1, 16),), jnp.float32),
        "obs_var": jnp.clip(jnp.exp(math.log(4.0) - 2.5902671 * jax.random.uniform(part_keys[2], (BATCHES, NOBS), jnp.float32) ** block_scale(part_keys[2], (BATCHES, NOBS), ((1, 16),), -0.2, 0.2)), 0.3, 4.0),
        "obs_site": place_ends(jax.random.randint(part_keys[3], (BATCHES, NOBS), 0, S_DEV), jax.random.fold_in(part_keys[3], 1), 0, S_DEV - 1).astype(jnp.int32),
        "loc_pattern": place_ends((jax.random.randint(part_keys[4], (BATCHES, NBLK, NTILE), 0, 2) < 1).astype(jnp.int32), jax.random.fold_in(part_keys[4], 1), 0, 1),
    }


EPS = 1e-05

def reference(ensemble, obs_value, obs_var, obs_site, loc_pattern):
    nblk = N_STATE * N_MEMBER
    state = ensemble.astype(jnp.float32).reshape(M, nblk, S_DEV).transpose(1, 0, 2)
    owner = jnp.arange(NOBS, dtype=jnp.int32) // OBS_DEV
    tile = jnp.arange(NOBS, dtype=jnp.int32) // OBS_TILE
    for batch in range(BATCHES):
        site = obs_site[batch]
        prior = state[owner, :, site]
        ymean = lax.optimization_barrier(jnp.mean(prior, axis=1, keepdims=True))
        yanom = prior - ymean
        spread = lax.optimization_barrier(jnp.sum(yanom * yanom, axis=1)) / (M - 1.0)
        ovar = obs_var[batch]
        oval = obs_value[batch]
        post_mean = (ymean[:, 0] * ovar + oval * spread) / (ovar + spread)
        shrink = jnp.sqrt(ovar / (ovar + spread))
        incr = (post_mean[:, None] + shrink[:, None] * yanom - prior).astype(jnp.bfloat16)
        yanom_b = yanom.astype(jnp.bfloat16)
        gain = 1.0 / ((M - 1.0) * (spread + EPS))
        local_weight = loc_pattern[batch][:, tile].astype(jnp.float32)

        def update(args):
            block, wrow = args
            xanom = (block - lax.optimization_barrier(jnp.mean(block, axis=0, keepdims=True))).astype(jnp.bfloat16)
            cov = jnp.dot(yanom_b, xanom, preferred_element_type=jnp.float32)
            weights = (cov * (gain * wrow)[:, None]).astype(jnp.bfloat16)
            delta = lax.dot_general(incr, weights, (((0,), (0,)), ((), ())), preferred_element_type=jnp.float32)
            return block + delta
        state = lax.map(update, (state, local_weight))
    return state.transpose(1, 0, 2).reshape(M, nblk * S_DEV).astype(jnp.bfloat16)
```

```python
import functools

import jax
import jax.numpy as jnp
from jax import lax
from jax.experimental import pallas as pl
from jax.experimental.pallas import tpu as pltpu
from jax.sharding import PartitionSpec as P

BATCHES = 6


EPS = 1e-05


def panel_from_prior(prior, ovar, oval):
    members = prior.shape[1]
    ymean = jnp.mean(prior, axis=1, keepdims=True)
    yanom = prior - ymean
    spread = jnp.sum(yanom * yanom, axis=1) / (members - 1.0)
    post_mean = (ymean[:, 0] * ovar + oval * spread) / (ovar + spread)
    shrink = jnp.sqrt(ovar / (ovar + spread))
    incr = (post_mean[:, None] + shrink[:, None] * yanom - prior).astype(jnp.bfloat16)
    gain = 1.0 / ((members - 1.0) * (spread + EPS))
    return (yanom.astype(jnp.bfloat16), incr, gain)


def apply_rows(total, xanom, yanom_b, incr, gain, wrow):
    cov = jnp.dot(yanom_b, xanom, preferred_element_type=jnp.float32)
    weights = (cov * (gain * wrow)[:, None]).astype(jnp.bfloat16)
    return total + lax.dot_general(
        incr, weights, (((0,), (0,)), ((), ())), preferred_element_type=jnp.float32
    )


def per_device(ensemble, obs_value, obs_var, obs_site, loc_pattern):
    gathered = lax.all_to_all(ensemble, "member", split_axis=1, concat_axis=0, tiled=True)
    state = gathered.astype(jnp.float32)
    members = gathered.shape[0]
    own_obs = obs_site.shape[1]
    nblocks = loc_pattern.shape[1] * lax.axis_size(("state", "member"))
    total_obs = own_obs * nblocks
    ntiles = loc_pattern.shape[2]
    obs_tile = total_obs // ntiles
    own_cols = jnp.take(gathered, obs_site.reshape(-1), axis=1)
    all_cols, all_loc = (
        lax.all_gather(own_cols, ("state", "member"), axis=1, tiled=True),
        lax.all_gather(loc_pattern.astype(jnp.bfloat16), ("state", "member"), axis=1, tiled=True),
    )
    all_vals, all_vars = (
        lax.all_gather(obs_value, ("state", "member"), axis=1, tiled=True),
        lax.all_gather(obs_var, ("state", "member"), axis=1, tiled=True),
    )
    columns = all_cols.astype(jnp.float32).reshape(members, nblocks, BATCHES, own_obs)
    columns = columns.transpose(2, 0, 1, 3).reshape(BATCHES, members, total_obs)
    col_block = jnp.arange(total_obs, dtype=jnp.int32) // own_obs
    block_onehot = (col_block[:, None] == jnp.arange(nblocks, dtype=jnp.int32)[None, :]).astype(
        jnp.float32
    )
    obs_tiles = jnp.arange(total_obs, dtype=jnp.int32) // obs_tile
    tile_onehot = (obs_tiles[:, None] == jnp.arange(ntiles, dtype=jnp.int32)[None, :]).astype(
        jnp.float32
    )
    for batch in range(BATCHES):
        prior = columns[batch].T
        yanom_b, incr, gain = panel_from_prior(prior, all_vars[batch], all_vals[batch])
        wrow = jnp.repeat(loc_pattern[batch, 0].astype(jnp.float32), obs_tile)
        xanom = (state - jnp.mean(state, axis=0, keepdims=True)).astype(jnp.bfloat16)
        state = apply_rows(state, xanom, yanom_b, incr, gain, wrow)
        if batch + 1 < BATCHES:
            later = columns[batch + 1 :].transpose(1, 0, 2).reshape(members, -1)
            col_anom = (later - jnp.mean(later, axis=0, keepdims=True)).astype(jnp.bfloat16)
            loc_now = all_loc[batch].astype(jnp.float32)
            col_loc = jnp.dot(
                jnp.dot(block_onehot, loc_now, precision=lax.Precision.HIGHEST),
                tile_onehot.T,
                precision=lax.Precision.HIGHEST,
            )
            wmat = jnp.tile(col_loc.T, (1, BATCHES - batch - 1))
            cov = jnp.dot(yanom_b, col_anom, preferred_element_type=jnp.float32)
            weights = (cov * gain[:, None] * wmat).astype(jnp.bfloat16)
            later = later + lax.dot_general(
                incr, weights, (((0,), (0,)), ((), ())), preferred_element_type=jnp.float32
            )
            later = later.reshape(members, BATCHES - batch - 1, total_obs).transpose(1, 0, 2)
            columns = jnp.concatenate([columns[: batch + 1], later], axis=0)
    return lax.all_to_all(
        state.astype(jnp.bfloat16), "member", split_axis=0, concat_axis=1, tiled=True
    )


LANES = 128
MESH = pl.DeviceIdType.MESH


def row_mean(values):
    return jnp.mean(values, axis=1, keepdims=True)


def ensemble_kernel(
    nz, own, ens_ref, meta_ref, out_ref,
    meta, cols, every, state, qstate, vals, lxs, qsend, qrecv,
    meta_s, meta_r, z_s, z_r, x_s, x_r, c_s, c_r, d_s, d_r,
    ex_s, ex_r, ec_s, ec_r, ed_s, ed_r, q_s, q_r, local_s,
):
    f32, bf16 = jnp.float32, jnp.bfloat16
    nm = 4
    rows, width = ens_ref.shape
    block = width // nm
    members = rows * nm
    nobs = nz * nm * own
    z, m = lax.axis_index("state"), lax.axis_index("member")

    def peer(dz, dm):
        return {"state": lax.rem(z + dz, nz), "member": jnp.bitwise_xor(m, dm)}

    def send(src, dst, ssem, rsem, dz, dm):
        copy = pltpu.make_async_remote_copy(
            src_ref=src, dst_ref=dst, send_sem=ssem, recv_sem=rsem,
            device_id=peer(dz, dm), device_id_type=MESH,
        )
        copy.start()
        sent.append(copy)
        return copy

    sent = []
    others = [(dz, dm) for dz in range(nz) for dm in range(nm) if dz or dm]
    barrier = pltpu.get_barrier_semaphore()
    for dz, dm in others:
        pl.semaphore_signal(barrier, inc=1, device_id=peer(dz, dm), device_id_type=MESH)
    pl.semaphore_wait(barrier, len(others))

    mine = z * nm + m
    meta[mine] = meta_ref[...]
    meta_copies = {}
    for dz, dm in others:
        at = dz * nm + dm
        meta_copies[dz, dm] = send(meta.at[mine], meta.at[mine], meta_s.at[at], meta_r.at[at], dz, dm)
    base = pl.multiple_of(m * rows, rows)
    base_x = pl.multiple_of(jnp.bitwise_xor(m, 2) * rows, rows)
    keep = pltpu.make_async_copy(ens_ref, every.at[pl.ds(base, rows), :], local_s)
    keep.start()
    for dm in range(1, nm):
        meta_copies[0, dm].wait_recv()

    site_iota = lax.broadcasted_iota(jnp.int32, (block, LANES), 0).astype(f32)
    first, second = [], []
    for kk in range(nm):
        got = meta[z * nm + kk]
        piece = ens_ref[:, kk * block : (kk + 1) * block]
        for out, r in ((first, 6), (second, 7)):
            onehot = jnp.where(site_iota == got[r : r + 1, :], 1.0, 0.0).astype(bf16)
            out.append(jnp.dot(piece, onehot, preferred_element_type=f32).astype(bf16))
    r_iota = lax.broadcasted_iota(jnp.int32, (nm * LANES, nm * LANES), 0)
    c_iota = lax.broadcasted_iota(jnp.int32, (nm * LANES, nm * LANES), 1)
    target = (r_iota % LANES) // own * LANES + r_iota // LANES * own + r_iota % own
    perm = jnp.where(c_iota == target, 1.0, 0.0).astype(bf16)
    placed = jnp.dot(jnp.concatenate(first, axis=1), perm, preferred_element_type=f32).astype(bf16)
    placed2 = jnp.dot(
        jnp.concatenate(second, axis=1), perm[:, : 2 * LANES], preferred_element_type=f32
    ).astype(bf16)
    cols[z, pl.ds(base, rows), 0 : nm * LANES] = placed
    cols[z, pl.ds(base, rows), nm * LANES : BATCHES * LANES] = placed2

    chunks = (pl.ds(0, LANES), pl.ds(LANES, (BATCHES - 1) * LANES))

    def view(d, c, start):
        return cols.at[lax.rem(z - d + nz, nz), pl.ds(start, rows), chunks[c]]

    zc, xc, cc, dc = {}, {}, {}, {}

    def forward(c, d):
        at = c * nz + d
        v = view(d, c, base)
        xc[c, d] = send(v, v, x_s.at[at], x_r.at[at], 0, 2)
        cc[c, d] = send(v, v, c_s.at[at], c_r.at[at], 0, 1)

    def relay(c, d):
        at = c * nz + d
        xc[c, d].wait_recv()
        v = view(d, c, base_x)
        dc[c, d] = send(v, v, d_s.at[at], d_r.at[at], 0, 1)

    for c in range(2):
        v = view(0, c, base)
        for d in range(1, nz):
            at = c * nz + d
            zc[c, d] = send(v, v, z_s.at[at], z_r.at[at], d, 0)
        forward(c, 0)

    for dz, dm in others:
        if dz:
            meta_copies[dz, dm].wait_recv()
    for k in range(nz * nm):
        turned = meta[k].T
        vals[0, k * own : (k + 1) * own, :] = turned[0:own, :]
        vals[1, k * own : (k + 1) * own, :] = turned[own : 2 * own, :]
    ntiles = 8
    er = lax.broadcasted_iota(jnp.int32, (LANES, nobs), 0)
    ec = lax.broadcasted_iota(jnp.int32, (LANES, nobs), 1)
    expand = jnp.where(er == ec // (nobs // ntiles) + 2 * own, 1.0, 0.0).astype(bf16)
    own_loc = jnp.dot(meta_ref[...].astype(bf16), expand, preferred_element_type=f32)
    wide = jnp.dot(
        meta[...].reshape(nz * nm * 8, LANES).astype(bf16), expand, preferred_element_type=f32
    ).reshape(nz * nm, 8, nobs)
    for b in range(BATCHES):
        lxs[b] = wide[:, b, :]

    for d in range(1, nz):
        zc[0, d].wait_recv()
        forward(0, d)
    for d in range(nz):
        relay(0, d)
    for d in range(1, nz):
        zc[1, d].wait_recv()
        forward(1, d)

    exc, ecc, edc = {}, {}, {}
    for kk in range(nm):
        part = pl.ds(kk * block, block)
        there = every.at[pl.ds(base, rows), part]
        exc[kk] = send(ens_ref.at[:, part], there, ex_s.at[kk], ex_r.at[kk], 0, 2)
        ecc[kk] = send(ens_ref.at[:, part], there, ec_s.at[kk], ec_r.at[kk], 0, 1)

    def relay_ens(kk):
        exc[kk].wait_recv()
        there = every.at[pl.ds(base_x, rows), pl.ds(kk * block, block)]
        edc[kk] = send(there, there, ed_s.at[kk], ed_r.at[kk], 0, 1)

    def arrive(c):
        for d in range(nz):
            cc[c, d].wait_recv()
            dc[c, d].wait_recv()

    def unpack(b):
        for zz in range(nz):
            got = cols[zz, :, b * LANES : (b + 1) * LANES].astype(f32)
            state[b, zz * LANES : (zz + 1) * LANES, :] = got.T

    qr = lax.broadcasted_iota(jnp.int32, (members, members), 0)
    qc = lax.broadcasted_iota(jnp.int32, (members, members), 1)
    eye = jnp.where(qr == qc, 1.0, 0.0)
    contract = (((1,), (1,)), ((), ()))

    arrive(0)
    unpack(0)
    for b in range(BATCHES):
        prior = state[b]
        ovar, oval = vals[1, :, b : b + 1], vals[0, :, b : b + 1]
        ymean = row_mean(prior)
        yanom = prior - ymean
        spread = jnp.sum(yanom * yanom, axis=1, keepdims=True) / (members - 1.0)
        post_mean = (ymean * ovar + oval * spread) / (ovar + spread)
        shrink = jnp.sqrt(ovar / (ovar + spread))
        incr = (post_mean + shrink * yanom - prior).astype(bf16)
        gain = 1.0 / ((members - 1.0) * (spread + EPS))
        ygain = (yanom * gain).astype(bf16)

        if b == 0:
            weights = (lax.dot_general(eye.astype(bf16), ygain, contract, preferred_element_type=f32)
                       * own_loc[0:1, :]).astype(bf16)
            qstate[...] = jnp.dot(weights, incr, preferred_element_type=f32)
            for d in range(nz):
                relay(1, d)
            arrive(1)
            for later in range(1, BATCHES):
                unpack(later)
        else:
            q = qstate[...]
            xanom = (q - row_mean(q) + eye).astype(bf16)
            weights = (lax.dot_general(xanom, ygain, contract, preferred_element_type=f32)
                       * own_loc[b : b + 1, :]).astype(bf16)
            qstate[...] = q + jnp.dot(weights, incr, preferred_element_type=f32)

        if b + 1 < BATCHES:
            local = lxs[b]

            @pl.loop(b + 1, BATCHES)
            def _(later):
                x = state[later]
                xanom = (x - row_mean(x)).astype(bf16)
                cov = lax.dot_general(xanom, ygain, contract, preferred_element_type=f32)
                cov = cov.reshape(nz * nm, own, nobs) * local[:, None, :]
                weights = cov.reshape(nobs, nobs).astype(bf16)
                state[later] = x + jnp.dot(weights, incr, preferred_element_type=f32)

        if 1 <= b <= nm - 1:
            relay_ens(b - 1)

    q = qstate[...]
    q = (q - jnp.mean(q, axis=0, keepdims=True)).T.astype(bf16)
    qsend[...] = q
    qrecv[m] = qsend[pl.ds(base, rows), :]
    qcs = []
    for dm in range(1, nm):
        to = pl.multiple_of(jnp.bitwise_xor(m, dm) * rows, rows)
        qcs.append(send(qsend.at[pl.ds(to, rows), :], qrecv.at[m], q_s.at[dm], q_r.at[dm], 0, dm))
    relay_ens(nm - 1)
    keep.wait()
    for copy in qcs:
        copy.wait_recv()
    for kk in range(nm):
        ecc[kk].wait_recv()
        edc[kk].wait_recv()
        part = slice(kk * block, (kk + 1) * block)
        delta = jnp.dot(qrecv[kk], every[:, part], preferred_element_type=f32)
        out_ref[:, part] = (ens_ref[:, part].astype(f32) + delta).astype(bf16)
    for copy in sent:
        copy.wait_send()


def per_device_kernel(nz, ensemble, obs_value, obs_var, obs_site, loc_pattern):
    nm = 4
    own = obs_site.shape[1]
    rows, width = ensemble.shape
    members, nobs, block = rows * nm, nz * nm * own, width // nm
    loc = loc_pattern[:, 0, :].astype(jnp.float32)
    head = jnp.concatenate([obs_value, obs_var, loc], axis=1)
    head = jnp.pad(head, ((0, 0), (0, LANES - head.shape[1])))
    sites = obs_site.astype(jnp.float32).reshape(-1)
    sites = jnp.pad(sites, (0, 2 * LANES - sites.shape[0]), constant_values=-1.0)
    meta = jnp.concatenate([head, sites.reshape(2, LANES)], axis=0)
    dma, bf16, f32 = pltpu.SemaphoreType.DMA, jnp.bfloat16, jnp.float32
    two = [dma((2 * nz,))] * 2
    return pl.pallas_call(
        functools.partial(ensemble_kernel, nz, own),
        out_shape=jax.ShapeDtypeStruct(ensemble.shape, bf16),
        in_specs=[pl.BlockSpec(memory_space=pltpu.VMEM)] * 2,
        out_specs=pl.BlockSpec(memory_space=pltpu.VMEM),
        scratch_shapes=[
            pltpu.VMEM((nz * nm, 8, LANES), f32),
            pltpu.VMEM((nz, members, BATCHES * LANES), bf16),
            pltpu.VMEM((members, width), bf16),
            pltpu.VMEM((BATCHES, nobs, members), f32),
            pltpu.VMEM((members, members), f32),
            pltpu.VMEM((2, nobs, 8), f32),
            pltpu.VMEM((BATCHES, nz * nm, nobs), f32),
            pltpu.VMEM((members, members), bf16),
            pltpu.VMEM((nm, rows, members), bf16),
            dma((nz * nm,)), dma((nz * nm,)),
            *two, *two, *two, *two,
            *[dma((nm,))] * 8,
            dma,
        ],
        compiler_params=pltpu.CompilerParams(
            collective_id=0, has_side_effects=True, vmem_limit_bytes=48 * 2**20
        ),
    )(ensemble, meta)


def dispatch(nz, nm, ensemble, obs_value, obs_var, obs_site, loc_pattern):
    own = obs_site.shape[1]
    fits = (
        nm == 4 and own * nm == LANES and obs_site.shape[0] == BATCHES and loc_pattern.shape[1:] == (1, 8)
        and ensemble.shape[0] % 16 == 0 and ensemble.shape[1] % (nm * LANES) == 0
    )
    if fits:
        return per_device_kernel(nz, ensemble, obs_value, obs_var, obs_site, loc_pattern)
    return per_device(ensemble, obs_value, obs_var, obs_site, loc_pattern)


def solution(mesh):
    in_specs = (
        P("member", ("groups", "state")),
        P(None, ("groups", "state", "member")),
        P(None, ("groups", "state", "member")),
        P(None, ("groups", "state", "member")),
        P(None, ("groups", "state", "member"), None),
    )
    out_specs = P("member", ("groups", "state"))
    sizes = (mesh.shape["state"], mesh.shape["member"])
    return jax.shard_map(
        functools.partial(dispatch, *sizes), mesh=mesh, in_specs=in_specs, out_specs=out_specs, check_vma=False
    )
```

```python
import functools

import jax
import jax.numpy as jnp
from jax import lax
from jax.experimental import pallas as pl
from jax.experimental.pallas import tpu as pltpu
from jax.sharding import PartitionSpec as P

BATCHES = 6


EPS = 1e-05


def panel_from_prior(prior, ovar, oval):
    members = prior.shape[1]
    ymean = jnp.mean(prior, axis=1, keepdims=True)
    yanom = prior - ymean
    spread = jnp.sum(yanom * yanom, axis=1) / (members - 1.0)
    post_mean = (ymean[:, 0] * ovar + oval * spread) / (ovar + spread)
    shrink = jnp.sqrt(ovar / (ovar + spread))
    incr = (post_mean[:, None] + shrink[:, None] * yanom - prior).astype(jnp.bfloat16)
    gain = 1.0 / ((members - 1.0) * (spread + EPS))
    return (yanom.astype(jnp.bfloat16), incr, gain)


def apply_rows(total, xanom, yanom_b, incr, gain, wrow):
    cov = jnp.dot(yanom_b, xanom, preferred_element_type=jnp.float32)
    weights = (cov * (gain * wrow)[:, None]).astype(jnp.bfloat16)
    return total + lax.dot_general(
        incr, weights, (((0,), (0,)), ((), ())), preferred_element_type=jnp.float32
    )


def per_device(ensemble, obs_value, obs_var, obs_site, loc_pattern):
    gathered = lax.all_to_all(ensemble, "member", split_axis=1, concat_axis=0, tiled=True)
    state = gathered.astype(jnp.float32)
    members = gathered.shape[0]
    own_obs = obs_site.shape[1]
    nblocks = loc_pattern.shape[1] * lax.axis_size(("state", "member"))
    total_obs = own_obs * nblocks
    ntiles = loc_pattern.shape[2]
    obs_tile = total_obs // ntiles
    own_cols = jnp.take(gathered, obs_site.reshape(-1), axis=1)
    all_cols, all_loc = (
        lax.all_gather(own_cols, ("state", "member"), axis=1, tiled=True),
        lax.all_gather(loc_pattern.astype(jnp.bfloat16), ("state", "member"), axis=1, tiled=True),
    )
    all_vals, all_vars = (
        lax.all_gather(obs_value, ("state", "member"), axis=1, tiled=True),
        lax.all_gather(obs_var, ("state", "member"), axis=1, tiled=True),
    )
    columns = all_cols.astype(jnp.float32).reshape(members, nblocks, BATCHES, own_obs)
    columns = columns.transpose(2, 0, 1, 3).reshape(BATCHES, members, total_obs)
    col_block = jnp.arange(total_obs, dtype=jnp.int32) // own_obs
    block_onehot = (col_block[:, None] == jnp.arange(nblocks, dtype=jnp.int32)[None, :]).astype(
        jnp.float32
    )
    obs_tiles = jnp.arange(total_obs, dtype=jnp.int32) // obs_tile
    tile_onehot = (obs_tiles[:, None] == jnp.arange(ntiles, dtype=jnp.int32)[None, :]).astype(
        jnp.float32
    )
    for batch in range(BATCHES):
        prior = columns[batch].T
        yanom_b, incr, gain = panel_from_prior(prior, all_vars[batch], all_vals[batch])
        wrow = jnp.repeat(loc_pattern[batch, 0].astype(jnp.float32), obs_tile)
        xanom = (state - jnp.mean(state, axis=0, keepdims=True)).astype(jnp.bfloat16)
        state = apply_rows(state, xanom, yanom_b, incr, gain, wrow)
        if batch + 1 < BATCHES:
            later = columns[batch + 1 :].transpose(1, 0, 2).reshape(members, -1)
            col_anom = (later - jnp.mean(later, axis=0, keepdims=True)).astype(jnp.bfloat16)
            loc_now = all_loc[batch].astype(jnp.float32)
            col_loc = jnp.dot(
                jnp.dot(block_onehot, loc_now, precision=lax.Precision.HIGHEST),
                tile_onehot.T,
                precision=lax.Precision.HIGHEST,
            )
            wmat = jnp.tile(col_loc.T, (1, BATCHES - batch - 1))
            cov = jnp.dot(yanom_b, col_anom, preferred_element_type=jnp.float32)
            weights = (cov * gain[:, None] * wmat).astype(jnp.bfloat16)
            later = later + lax.dot_general(
                incr, weights, (((0,), (0,)), ((), ())), preferred_element_type=jnp.float32
            )
            later = later.reshape(members, BATCHES - batch - 1, total_obs).transpose(1, 0, 2)
            columns = jnp.concatenate([columns[: batch + 1], later], axis=0)
    return lax.all_to_all(
        state.astype(jnp.bfloat16), "member", split_axis=0, concat_axis=1, tiled=True
    )


LANES = 128
MESH = pl.DeviceIdType.MESH


def row_mean(values):
    return jnp.mean(values, axis=1, keepdims=True)


def ensemble_kernel(
    nz, own, ens_ref, val_ref, var_ref, site_ref, loc_ref, out_ref,
    meta, cols, every, state, ygains, incrs, qstate, vals, lxs, qsend, qrecv,
    val_in, var_in, site_in, loc_in,
    meta_s, meta_r, z_s, z_r, x_s, x_r, c_s, c_r,
    ex_s, ex_r, ec_s, ec_r, ed_s, ed_r, q_s, q_r, local_s,
):
    f32, bf16 = jnp.float32, jnp.bfloat16
    nm = 4
    rows, width = ens_ref.shape
    block = width // nm
    members = rows * nm
    nobs = nz * nm * own
    z, m = lax.axis_index("state"), lax.axis_index("member")

    def peer(dz, dm):
        return {"state": lax.rem(z + dz, nz), "member": jnp.bitwise_xor(m, dm)}

    def send(src, dst, ssem, rsem, dz, dm):
        copy = pltpu.make_async_remote_copy(
            src_ref=src, dst_ref=dst, send_sem=ssem, recv_sem=rsem,
            device_id=peer(dz, dm), device_id_type=MESH,
        )
        copy.start()
        sent.append(copy)
        return copy

    def place(member):
        return pl.multiple_of((member % 2 * 2 + member // 2) * rows, rows)

    base = place(m)
    pair = pl.multiple_of(m % 2 * (2 * rows), 2 * rows)
    pair_c = pl.multiple_of((1 - m % 2) * (2 * rows), 2 * rows)
    base_x = place(jnp.bitwise_xor(m, 2))
    loads = [
        pltpu.make_async_copy(src, dst, local_s.at[at])
        for at, (src, dst) in enumerate((
            (val_ref, val_in), (var_ref, var_in), (site_ref, site_in), (loc_ref, loc_in),
            (ens_ref, every.at[pl.ds(base, rows), :]),
        ))
    ]
    for copy in loads:
        copy.start()

    sent = []
    others = [(dz, dm) for dz in range(nz) for dm in range(nm) if dz or dm]
    barrier = pltpu.get_barrier_semaphore()
    for dz, dm in others:
        pl.semaphore_signal(barrier, inc=1, device_id=peer(dz, dm), device_id_type=MESH)
    for copy in loads[:4]:
        copy.wait()
    mine = z * nm + m
    loc = loc_in[:, 0, :].astype(f32)
    sites = [site_in[b : b + 1, :].astype(f32) for b in range(BATCHES)]
    spare = LANES - 2 * own - loc.shape[1]
    meta[mine, 0:BATCHES, :] = jnp.concatenate(
        [val_in[...], var_in[...], loc, jnp.zeros((BATCHES, spare), f32)], axis=1
    )
    meta[mine, 6:7, :] = jnp.concatenate(sites[:4], axis=1)
    meta[mine, 7:8, :] = jnp.concatenate(
        sites[4:] + [jnp.full((1, LANES - 2 * own), -1.0, f32)], axis=1
    )
    pl.semaphore_wait(barrier, len(others))
    meta_copies = {}
    for dz, dm in others:
        at = dz * nm + dm
        meta_copies[dz, dm] = send(meta.at[mine], meta.at[mine], meta_s.at[at], meta_r.at[at], dz, dm)
    loads[4].wait()
    exc, ecc, edc = {}, {}, {}

    def send_ens(kk):
        there = every.at[pl.ds(base, rows), pl.ds(kk * block, block)]
        exc[kk] = send(there, there, ex_s.at[kk], ex_r.at[kk], 0, 2)
        ecc[kk] = send(there, there, ec_s.at[kk], ec_r.at[kk], 0, 1)

    def relay_ens(kk):
        exc[kk].wait_recv()
        there = every.at[pl.ds(base_x, rows), pl.ds(kk * block, block)]
        edc[kk] = send(there, there, ed_s.at[kk], ed_r.at[kk], 0, 1)

    send_ens(0)
    for dm in range(1, nm):
        meta_copies[0, dm].wait_recv()

    site_iota = lax.broadcasted_iota(jnp.int32, (block, LANES), 0).astype(f32)
    first, second = [], []
    for kk in range(nm):
        got = meta[z * nm + kk]
        piece = every[pl.ds(base, rows), kk * block : (kk + 1) * block]
        for out, r in ((first, 6), (second, 7)):
            onehot = jnp.where(site_iota == got[r : r + 1, :], 1.0, 0.0).astype(bf16)
            out.append(jnp.dot(piece, onehot, preferred_element_type=f32).astype(bf16))
    r_iota = lax.broadcasted_iota(jnp.int32, (nm * LANES, nm * LANES), 0)
    c_iota = lax.broadcasted_iota(jnp.int32, (nm * LANES, nm * LANES), 1)
    target = (r_iota % LANES) // own * LANES + r_iota // LANES * own + r_iota % own
    perm = jnp.where(c_iota == target, 1.0, 0.0).astype(bf16)
    placed = jnp.dot(jnp.concatenate(first, axis=1), perm, preferred_element_type=f32).astype(bf16)
    placed2 = jnp.dot(
        jnp.concatenate(second, axis=1), perm[:, : 2 * LANES], preferred_element_type=f32
    ).astype(bf16)
    cols[z, pl.ds(base, rows), 0 : nm * LANES] = placed
    cols[z, pl.ds(base, rows), nm * LANES : BATCHES * LANES] = placed2

    chunks = ((0, 1), (1, 3), (3, BATCHES))

    def view(d, c, start, count):
        low, high = chunks[c]
        lanes = pl.ds(low * LANES, (high - low) * LANES)
        return cols.at[lax.rem(z - d + nz, nz), pl.ds(start, count), lanes]

    zc, xc, cc = {}, {}, {}

    def go_z(c, start, count):
        v = view(0, c, start, count)
        for d in range(1, nz):
            at = c * nz + d
            zc[c, d] = send(v, v, z_s.at[at], z_r.at[at], d, 0)

    def go_x(c, d):
        at, v = c * nz + d, view(d, c, base, rows)
        xc[c, d] = send(v, v, x_s.at[at], x_r.at[at], 0, 2)

    def go_core(c, d):
        at, v = c * nz + d, view(d, c, pair, 2 * rows)
        cc[c, d] = send(v, v, c_s.at[at], c_r.at[at], 0, 1)

    def arrive(c):
        for d in range(nz):
            cc[c, d].wait_recv()

    go_x(0, 0)
    go_x(2, 0)
    go_x(1, 0)
    xc[0, 0].wait_recv()
    go_z(0, pair, 2 * rows)
    go_core(0, 0)
    go_z(1, base, rows)
    xc[2, 0].wait_recv()
    go_z(2, pair, 2 * rows)
    go_core(2, 0)

    for dz, dm in others:
        if dz:
            meta_copies[dz, dm].wait_recv()
    for k in range(nz * nm):
        turned = meta[k].T
        vals[0, k * own : (k + 1) * own, :] = turned[0:own, :]
        vals[1, k * own : (k + 1) * own, :] = turned[own : 2 * own, :]
    ntiles = 8
    er = lax.broadcasted_iota(jnp.int32, (LANES, nobs), 0)
    ec = lax.broadcasted_iota(jnp.int32, (LANES, nobs), 1)
    expand = jnp.where(er == ec // (nobs // ntiles) + 2 * own, 1.0, 0.0).astype(bf16)
    own_loc = jnp.dot(meta[mine].astype(bf16), expand, preferred_element_type=f32)
    wide = jnp.dot(
        meta[...].reshape(nz * nm * 8, LANES).astype(bf16), expand, preferred_element_type=f32
    ).reshape(nz * nm, 8, nobs)
    for b in range(BATCHES):
        lxs[b] = wide[:, b, :]

    for d in range(1, nz):
        zc[0, d].wait_recv()
        go_core(0, d)
    for d in range(1, nz):
        zc[1, d].wait_recv()
        go_x(1, d)
    for kk in range(1, nm):
        send_ens(kk)

    def unpack(b):
        for zz in range(nz):
            got = cols[zz, :, b * LANES : (b + 1) * LANES].astype(f32)
            state[b, zz * LANES : (zz + 1) * LANES, :] = got.T

    qr = lax.broadcasted_iota(jnp.int32, (members, members), 0)
    qc = lax.broadcasted_iota(jnp.int32, (members, members), 1)
    eye = jnp.where(qr == qc, 1.0, 0.0)
    contract = (((1,), (1,)), ((), ()))

    for b in range(BATCHES):
        for c, (low, high) in enumerate(chunks):
            if b == low:
                if c == 1:
                    for d in range(nz):
                        xc[1, d].wait_recv()
                        go_core(1, d)
                if c == 2:
                    for d in range(1, nz):
                        zc[2, d].wait_recv()
                        go_core(2, d)
                    relay_ens(0)
                arrive(c)
                for fresh in range(low, high):
                    unpack(fresh)

        if b:
            @pl.loop(0, b)
            def _(earlier):
                x = state[b]
                xanom = (x - row_mean(x)).astype(bf16)
                cov = lax.dot_general(xanom, ygains[earlier], contract, preferred_element_type=f32)
                cov = cov.reshape(nz * nm, own, nobs) * lxs[earlier][:, None, :]
                weights = cov.reshape(nobs, nobs).astype(bf16)
                state[b] = x + jnp.dot(weights, incrs[earlier], preferred_element_type=f32)

        prior = state[b]
        ovar, oval = vals[1, :, b : b + 1], vals[0, :, b : b + 1]
        ymean = row_mean(prior)
        yanom = prior - ymean
        spread = jnp.sum(yanom * yanom, axis=1, keepdims=True) / (members - 1.0)
        post_mean = (ymean * ovar + oval * spread) / (ovar + spread)
        shrink = jnp.sqrt(ovar / (ovar + spread))
        incr = (post_mean + shrink * yanom - prior).astype(bf16)
        gain = 1.0 / ((members - 1.0) * (spread + EPS))
        ygain = (yanom * gain).astype(bf16)
        if b + 1 < BATCHES:
            ygains[b] = ygain
            incrs[b] = incr

        if b == 0:
            weights = (lax.dot_general(eye.astype(bf16), ygain, contract, preferred_element_type=f32)
                       * own_loc[0:1, :]).astype(bf16)
            qstate[...] = jnp.dot(weights, incr, preferred_element_type=f32)
        else:
            q = qstate[...]
            xanom = (q - row_mean(q) + eye).astype(bf16)
            weights = (lax.dot_general(xanom, ygain, contract, preferred_element_type=f32)
                       * own_loc[b : b + 1, :]).astype(bf16)
            qstate[...] = q + jnp.dot(weights, incr, preferred_element_type=f32)
        if b >= 4:
            relay_ens(b - 3)

    q = qstate[...]
    q = (q - jnp.mean(q, axis=0, keepdims=True)).T.astype(bf16)
    qsend[...] = q
    qrecv[m] = qsend[pl.ds(base, rows), :]
    qcs = []
    for dm in range(1, nm):
        to = place(jnp.bitwise_xor(m, dm))
        qcs.append(send(qsend.at[pl.ds(to, rows), :], qrecv.at[m], q_s.at[dm], q_r.at[dm], 0, dm))
    relay_ens(nm - 1)
    for copy in qcs:
        copy.wait_recv()
    for kk in range(nm):
        ecc[kk].wait_recv()
        edc[kk].wait_recv()
        part = slice(kk * block, (kk + 1) * block)
        delta = jnp.dot(qrecv[kk], every[:, part], preferred_element_type=f32)
        out_ref[:, part] = (every[pl.ds(base, rows), part].astype(f32) + delta).astype(bf16)
    for copy in sent:
        copy.wait_send()


def per_device_kernel(nz, ensemble, obs_value, obs_var, obs_site, loc_pattern):
    nm = 4
    own = obs_site.shape[1]
    rows, width = ensemble.shape
    members, nobs, block = rows * nm, nz * nm * own, width // nm
    dma, bf16, f32 = pltpu.SemaphoreType.DMA, jnp.bfloat16, jnp.float32
    two = [dma((3 * nz,))] * 2
    return pl.pallas_call(
        functools.partial(ensemble_kernel, nz, own),
        out_shape=jax.ShapeDtypeStruct(ensemble.shape, bf16),
        in_specs=[pl.BlockSpec(memory_space=pl.ANY)] * 5,
        out_specs=pl.BlockSpec(memory_space=pltpu.VMEM),
        scratch_shapes=[
            pltpu.VMEM((nz * nm, 8, LANES), f32),
            pltpu.VMEM((nz, members, BATCHES * LANES), bf16),
            pltpu.VMEM((members, width), bf16),
            pltpu.VMEM((BATCHES, nobs, members), f32),
            pltpu.VMEM((BATCHES - 1, nobs, members), bf16),
            pltpu.VMEM((BATCHES - 1, nobs, members), bf16),
            pltpu.VMEM((members, members), f32),
            pltpu.VMEM((2, nobs, 8), f32),
            pltpu.VMEM((BATCHES, nz * nm, nobs), f32),
            pltpu.VMEM((members, members), bf16),
            pltpu.VMEM((nm, rows, members), bf16),
            pltpu.VMEM(obs_value.shape, f32),
            pltpu.VMEM(obs_var.shape, f32),
            pltpu.VMEM(obs_site.shape, jnp.int32),
            pltpu.VMEM(loc_pattern.shape, jnp.int32),
            dma((nz * nm,)), dma((nz * nm,)),
            *two, *two, *two,
            *[dma((nm,))] * 8,
            dma((5,)),
        ],
        compiler_params=pltpu.CompilerParams(
            collective_id=0, has_side_effects=True, vmem_limit_bytes=56 * 2**20
        ),
    )(ensemble, obs_value, obs_var, obs_site, loc_pattern)


def dispatch(nz, nm, ensemble, obs_value, obs_var, obs_site, loc_pattern):
    own = obs_site.shape[1]
    fits = (
        nm == 4 and own * nm == LANES and obs_site.shape[0] == BATCHES and loc_pattern.shape[1:] == (1, 8)
        and ensemble.shape[0] % 16 == 0 and ensemble.shape[1] % (nm * LANES) == 0
    )
    if fits:
        return per_device_kernel(nz, ensemble, obs_value, obs_var, obs_site, loc_pattern)
    return per_device(ensemble, obs_value, obs_var, obs_site, loc_pattern)


def solution(mesh):
    in_specs = (
        P("member", ("groups", "state")),
        P(None, ("groups", "state", "member")),
        P(None, ("groups", "state", "member")),
        P(None, ("groups", "state", "member")),
        P(None, ("groups", "state", "member"), None),
    )
    out_specs = P("member", ("groups", "state"))
    sizes = (mesh.shape["state"], mesh.shape["member"])
    return jax.shard_map(
        functools.partial(dispatch, *sizes), mesh=mesh, in_specs=in_specs, out_specs=out_specs, check_vma=False
    )
```

```python
import functools

import jax
import jax.numpy as jnp
from jax import lax
from jax.experimental import pallas as pl
from jax.experimental.pallas import tpu as pltpu
from jax.sharding import PartitionSpec as P

BATCHES = 6


EPS = 1e-05


def panel_from_prior(prior, ovar, oval):
    members = prior.shape[1]
    ymean = jnp.mean(prior, axis=1, keepdims=True)
    yanom = prior - ymean
    spread = jnp.sum(yanom * yanom, axis=1) / (members - 1.0)
    post_mean = (ymean[:, 0] * ovar + oval * spread) / (ovar + spread)
    shrink = jnp.sqrt(ovar / (ovar + spread))
    incr = (post_mean[:, None] + shrink[:, None] * yanom - prior).astype(jnp.bfloat16)
    gain = 1.0 / ((members - 1.0) * (spread + EPS))
    return (yanom.astype(jnp.bfloat16), incr, gain)


def apply_rows(total, xanom, yanom_b, incr, gain, wrow):
    cov = jnp.dot(yanom_b, xanom, preferred_element_type=jnp.float32)
    weights = (cov * (gain * wrow)[:, None]).astype(jnp.bfloat16)
    return total + lax.dot_general(
        incr, weights, (((0,), (0,)), ((), ())), preferred_element_type=jnp.float32
    )


def per_device(ensemble, obs_value, obs_var, obs_site, loc_pattern):
    gathered = lax.all_to_all(ensemble, "member", split_axis=1, concat_axis=0, tiled=True)
    state = gathered.astype(jnp.float32)
    members = gathered.shape[0]
    own_obs = obs_site.shape[1]
    nblocks = loc_pattern.shape[1] * lax.axis_size(("state", "member"))
    total_obs = own_obs * nblocks
    ntiles = loc_pattern.shape[2]
    obs_tile = total_obs // ntiles
    own_cols = jnp.take(gathered, obs_site.reshape(-1), axis=1)
    all_cols, all_loc = (
        lax.all_gather(own_cols, ("state", "member"), axis=1, tiled=True),
        lax.all_gather(loc_pattern.astype(jnp.bfloat16), ("state", "member"), axis=1, tiled=True),
    )
    all_vals, all_vars = (
        lax.all_gather(obs_value, ("state", "member"), axis=1, tiled=True),
        lax.all_gather(obs_var, ("state", "member"), axis=1, tiled=True),
    )
    columns = all_cols.astype(jnp.float32).reshape(members, nblocks, BATCHES, own_obs)
    columns = columns.transpose(2, 0, 1, 3).reshape(BATCHES, members, total_obs)
    col_block = jnp.arange(total_obs, dtype=jnp.int32) // own_obs
    block_onehot = (col_block[:, None] == jnp.arange(nblocks, dtype=jnp.int32)[None, :]).astype(
        jnp.float32
    )
    obs_tiles = jnp.arange(total_obs, dtype=jnp.int32) // obs_tile
    tile_onehot = (obs_tiles[:, None] == jnp.arange(ntiles, dtype=jnp.int32)[None, :]).astype(
        jnp.float32
    )
    for batch in range(BATCHES):
        prior = columns[batch].T
        yanom_b, incr, gain = panel_from_prior(prior, all_vars[batch], all_vals[batch])
        wrow = jnp.repeat(loc_pattern[batch, 0].astype(jnp.float32), obs_tile)
        xanom = (state - jnp.mean(state, axis=0, keepdims=True)).astype(jnp.bfloat16)
        state = apply_rows(state, xanom, yanom_b, incr, gain, wrow)
        if batch + 1 < BATCHES:
            later = columns[batch + 1 :].transpose(1, 0, 2).reshape(members, -1)
            col_anom = (later - jnp.mean(later, axis=0, keepdims=True)).astype(jnp.bfloat16)
            loc_now = all_loc[batch].astype(jnp.float32)
            col_loc = jnp.dot(
                jnp.dot(block_onehot, loc_now, precision=lax.Precision.HIGHEST),
                tile_onehot.T,
                precision=lax.Precision.HIGHEST,
            )
            wmat = jnp.tile(col_loc.T, (1, BATCHES - batch - 1))
            cov = jnp.dot(yanom_b, col_anom, preferred_element_type=jnp.float32)
            weights = (cov * gain[:, None] * wmat).astype(jnp.bfloat16)
            later = later + lax.dot_general(
                incr, weights, (((0,), (0,)), ((), ())), preferred_element_type=jnp.float32
            )
            later = later.reshape(members, BATCHES - batch - 1, total_obs).transpose(1, 0, 2)
            columns = jnp.concatenate([columns[: batch + 1], later], axis=0)
    return lax.all_to_all(
        state.astype(jnp.bfloat16), "member", split_axis=0, concat_axis=1, tiled=True
    )


LANES = 128
MESH = pl.DeviceIdType.MESH


def row_mean(values):
    return jnp.mean(values, axis=1, keepdims=True)


def ensemble_kernel(
    nz, own, ens_ref, val_ref, var_ref, site_ref, loc_ref, out_ref,
    meta, cols, every, state, ygains, incrs, qstate, vals, lxs, qsend, qrecv,
    val_in, var_in, site_in, loc_in,
    meta_s, meta_r, z_s, z_r, x_s, x_r, c_s, c_r,
    ex_s, ex_r, ec_s, ec_r, ed_s, ed_r, q_s, q_r, local_s,
):
    f32, bf16 = jnp.float32, jnp.bfloat16
    nm = 4
    rows, width = ens_ref.shape
    block = width // nm
    members = rows * nm
    nobs = nz * nm * own
    z, m = lax.axis_index("state"), lax.axis_index("member")

    def peer(dz, dm):
        return {"state": lax.rem(z + dz, nz), "member": jnp.bitwise_xor(m, dm)}

    def send(src, dst, ssem, rsem, dz, dm):
        copy = pltpu.make_async_remote_copy(
            src_ref=src, dst_ref=dst, send_sem=ssem, recv_sem=rsem,
            device_id=peer(dz, dm), device_id_type=MESH,
        )
        copy.start()
        sent.append(copy)
        return copy

    def place(member):
        return pl.multiple_of((member % 2 * 2 + member // 2) * rows, rows)

    base = place(m)
    pair = pl.multiple_of(m % 2 * (2 * rows), 2 * rows)
    pair_c = pl.multiple_of((1 - m % 2) * (2 * rows), 2 * rows)
    base_x = place(jnp.bitwise_xor(m, 2))
    loads = [
        pltpu.make_async_copy(src, dst, local_s.at[at])
        for at, (src, dst) in enumerate((
            (val_ref, val_in), (var_ref, var_in), (site_ref, site_in), (loc_ref, loc_in),
            (ens_ref, every.at[pl.ds(base, rows), :]),
        ))
    ]
    for copy in loads:
        copy.start()

    sent = []
    others = [(dz, dm) for dz in range(nz) for dm in range(nm) if dz or dm]
    barrier = pltpu.get_barrier_semaphore()
    for dz, dm in others:
        pl.semaphore_signal(barrier, inc=1, device_id=peer(dz, dm), device_id_type=MESH)
    for copy in loads[:4]:
        copy.wait()
    mine = z * nm + m
    loc = loc_in[:, 0, :].astype(f32)
    sites = [site_in[b : b + 1, :].astype(f32) for b in range(BATCHES)]
    spare = LANES - 2 * own - loc.shape[1]
    meta[mine, 0:BATCHES, :] = jnp.concatenate(
        [val_in[...], var_in[...], loc, jnp.zeros((BATCHES, spare), f32)], axis=1
    )
    meta[mine, 6:7, :] = jnp.concatenate(sites[:4], axis=1)
    meta[mine, 7:8, :] = jnp.concatenate(
        sites[4:] + [jnp.full((1, LANES - 2 * own), -1.0, f32)], axis=1
    )
    pl.semaphore_wait(barrier, len(others))
    meta_copies = {}
    for dz, dm in others:
        at = dz * nm + dm
        meta_copies[dz, dm] = send(meta.at[mine], meta.at[mine], meta_s.at[at], meta_r.at[at], dz, dm)
    loads[4].wait()
    exc, ecc, edc = {}, {}, {}

    def send_ens(kk):
        there = every.at[pl.ds(base, rows), pl.ds(kk * block, block)]
        exc[kk] = send(there, there, ex_s.at[kk], ex_r.at[kk], 0, 2)
        ecc[kk] = send(there, there, ec_s.at[kk], ec_r.at[kk], 0, 1)

    def relay_ens(kk):
        exc[kk].wait_recv()
        there = every.at[pl.ds(base_x, rows), pl.ds(kk * block, block)]
        edc[kk] = send(there, there, ed_s.at[kk], ed_r.at[kk], 0, 1)

    send_ens(0)
    for dm in range(1, nm):
        meta_copies[0, dm].wait_recv()

    site_iota = lax.broadcasted_iota(jnp.int32, (block, LANES), 0).astype(f32)
    first, second = [], []
    for kk in range(nm):
        got = meta[z * nm + kk]
        piece = every[pl.ds(base, rows), kk * block : (kk + 1) * block]
        for out, r in ((first, 6), (second, 7)):
            onehot = jnp.where(site_iota == got[r : r + 1, :], 1.0, 0.0).astype(bf16)
            out.append(jnp.dot(piece, onehot, preferred_element_type=f32).astype(bf16))
    r_iota = lax.broadcasted_iota(jnp.int32, (nm * LANES, nm * LANES), 0)
    c_iota = lax.broadcasted_iota(jnp.int32, (nm * LANES, nm * LANES), 1)
    target = (r_iota % LANES) // own * LANES + r_iota // LANES * own + r_iota % own
    perm = jnp.where(c_iota == target, 1.0, 0.0).astype(bf16)
    placed = jnp.dot(jnp.concatenate(first, axis=1), perm, preferred_element_type=f32).astype(bf16)
    placed2 = jnp.dot(
        jnp.concatenate(second, axis=1), perm[:, : 2 * LANES], preferred_element_type=f32
    ).astype(bf16)
    cols[z, pl.ds(base, rows), 0 : nm * LANES] = placed
    cols[z, pl.ds(base, rows), nm * LANES : BATCHES * LANES] = placed2

    chunks = ((0, 1), (1, 3), (3, BATCHES))

    def view(d, c, start, count):
        low, high = chunks[c]
        lanes = pl.ds(low * LANES, (high - low) * LANES)
        return cols.at[lax.rem(z - d + nz, nz), pl.ds(start, count), lanes]

    zc, xc, cc = {}, {}, {}

    def go_z(c, start, count):
        v = view(0, c, start, count)
        for d in range(1, nz):
            at = c * nz + d
            zc[c, d] = send(v, v, z_s.at[at], z_r.at[at], d, 0)

    def go_x(c, d):
        at, v = c * nz + d, view(d, c, base, rows)
        xc[c, d] = send(v, v, x_s.at[at], x_r.at[at], 0, 2)

    def go_core(c, d):
        at, v = c * nz + d, view(d, c, pair, 2 * rows)
        cc[c, d] = send(v, v, c_s.at[at], c_r.at[at], 0, 1)

    def arrive(c):
        for d in range(nz):
            cc[c, d].wait_recv()

    go_x(0, 0)
    go_x(2, 0)
    go_x(1, 0)
    xc[0, 0].wait_recv()
    go_z(0, pair, 2 * rows)
    go_core(0, 0)
    go_z(1, base, rows)

    for dz, dm in others:
        if dz:
            meta_copies[dz, dm].wait_recv()
    for k in range(nz * nm):
        turned = meta[k].T
        vals[0, k * own : (k + 1) * own, :] = turned[0:own, :]
        vals[1, k * own : (k + 1) * own, :] = turned[own : 2 * own, :]
    ntiles = 8
    er = lax.broadcasted_iota(jnp.int32, (LANES, nobs), 0)
    ec = lax.broadcasted_iota(jnp.int32, (LANES, nobs), 1)
    expand = jnp.where(er == ec // (nobs // ntiles) + 2 * own, 1.0, 0.0).astype(bf16)
    own_loc = jnp.dot(meta[mine].astype(bf16), expand, preferred_element_type=f32)
    wide = jnp.dot(
        meta[...].reshape(nz * nm * 8, LANES).astype(bf16), expand, preferred_element_type=f32
    ).reshape(nz * nm, 8, nobs)
    for b in range(BATCHES):
        lxs[b] = wide[:, b, :]

    for d in range(1, nz):
        zc[0, d].wait_recv()
        go_core(0, d)
    for d in range(1, nz):
        zc[1, d].wait_recv()
        go_x(1, d)
    xc[2, 0].wait_recv()
    go_z(2, pair, 2 * rows)
    go_core(2, 0)
    for kk in range(1, nm):
        send_ens(kk)

    def unpack(b):
        for zz in range(nz):
            got = cols[zz, :, b * LANES : (b + 1) * LANES].astype(f32)
            state[b, zz * LANES : (zz + 1) * LANES, :] = got.T

    qr = lax.broadcasted_iota(jnp.int32, (members, members), 0)
    qc = lax.broadcasted_iota(jnp.int32, (members, members), 1)
    eye = jnp.where(qr == qc, 1.0, 0.0)
    contract = (((1,), (1,)), ((), ()))

    for b in range(BATCHES):
        for c, (low, high) in enumerate(chunks):
            if b == low:
                if c == 1:
                    for d in range(nz):
                        xc[1, d].wait_recv()
                        go_core(1, d)
                if c == 2:
                    for d in range(1, nz):
                        zc[2, d].wait_recv()
                        go_core(2, d)
                    relay_ens(0)
                arrive(c)
                for fresh in range(low, high):
                    unpack(fresh)

        if b:
            @pl.loop(0, b)
            def _(earlier):
                x = state[b]
                xanom = (x - row_mean(x)).astype(bf16)
                cov = lax.dot_general(xanom, ygains[earlier], contract, preferred_element_type=f32)
                cov = cov.reshape(nz * nm, own, nobs) * lxs[earlier][:, None, :]
                weights = cov.reshape(nobs, nobs).astype(bf16)
                state[b] = x + jnp.dot(weights, incrs[earlier], preferred_element_type=f32)

        prior = state[b]
        ovar, oval = vals[1, :, b : b + 1], vals[0, :, b : b + 1]
        ymean = row_mean(prior)
        yanom = prior - ymean
        spread = jnp.sum(yanom * yanom, axis=1, keepdims=True) / (members - 1.0)
        post_mean = (ymean * ovar + oval * spread) / (ovar + spread)
        shrink = jnp.sqrt(ovar / (ovar + spread))
        incr = (post_mean + shrink * yanom - prior).astype(bf16)
        gain = 1.0 / ((members - 1.0) * (spread + EPS))
        ygain = (yanom * gain).astype(bf16)
        if b + 1 < BATCHES:
            ygains[b] = ygain
            incrs[b] = incr

        if b == 0:
            weights = (lax.dot_general(eye.astype(bf16), ygain, contract, preferred_element_type=f32)
                       * own_loc[0:1, :]).astype(bf16)
            qstate[...] = jnp.dot(weights, incr, preferred_element_type=f32)
        else:
            q = qstate[...]
            xanom = (q - row_mean(q) + eye).astype(bf16)
            weights = (lax.dot_general(xanom, ygain, contract, preferred_element_type=f32)
                       * own_loc[b : b + 1, :]).astype(bf16)
            qstate[...] = q + jnp.dot(weights, incr, preferred_element_type=f32)
        if b >= 4:
            relay_ens(b - 3)

    q = qstate[...]
    q = (q - jnp.mean(q, axis=0, keepdims=True)).T.astype(bf16)
    qsend[...] = q
    qrecv[m] = qsend[pl.ds(base, rows), :]
    qcs = []
    for dm in range(1, nm):
        to = place(jnp.bitwise_xor(m, dm))
        qcs.append(send(qsend.at[pl.ds(to, rows), :], qrecv.at[m], q_s.at[dm], q_r.at[dm], 0, dm))
    relay_ens(nm - 1)
    for copy in qcs:
        copy.wait_recv()
    for kk in range(nm):
        ecc[kk].wait_recv()
        edc[kk].wait_recv()
        part = slice(kk * block, (kk + 1) * block)
        delta = jnp.dot(qrecv[kk], every[:, part], preferred_element_type=f32)
        out_ref[:, part] = (every[pl.ds(base, rows), part].astype(f32) + delta).astype(bf16)
    for copy in sent:
        copy.wait_send()


def per_device_kernel(nz, ensemble, obs_value, obs_var, obs_site, loc_pattern):
    nm = 4
    own = obs_site.shape[1]
    rows, width = ensemble.shape
    members, nobs, block = rows * nm, nz * nm * own, width // nm
    dma, bf16, f32 = pltpu.SemaphoreType.DMA, jnp.bfloat16, jnp.float32
    two = [dma((3 * nz,))] * 2
    return pl.pallas_call(
        functools.partial(ensemble_kernel, nz, own),
        out_shape=jax.ShapeDtypeStruct(ensemble.shape, bf16),
        in_specs=[pl.BlockSpec(memory_space=pl.ANY)] * 5,
        out_specs=pl.BlockSpec(memory_space=pltpu.VMEM),
        scratch_shapes=[
            pltpu.VMEM((nz * nm, 8, LANES), f32),
            pltpu.VMEM((nz, members, BATCHES * LANES), bf16),
            pltpu.VMEM((members, width), bf16),
            pltpu.VMEM((BATCHES, nobs, members), f32),
            pltpu.VMEM((BATCHES - 1, nobs, members), bf16),
            pltpu.VMEM((BATCHES - 1, nobs, members), bf16),
            pltpu.VMEM((members, members), f32),
            pltpu.VMEM((2, nobs, 8), f32),
            pltpu.VMEM((BATCHES, nz * nm, nobs), f32),
            pltpu.VMEM((members, members), bf16),
            pltpu.VMEM((nm, rows, members), bf16),
            pltpu.VMEM(obs_value.shape, f32),
            pltpu.VMEM(obs_var.shape, f32),
            pltpu.VMEM(obs_site.shape, jnp.int32),
            pltpu.VMEM(loc_pattern.shape, jnp.int32),
            dma((nz * nm,)), dma((nz * nm,)),
            *two, *two, *two,
            *[dma((nm,))] * 8,
            dma((5,)),
        ],
        compiler_params=pltpu.CompilerParams(
            collective_id=0, has_side_effects=True, vmem_limit_bytes=56 * 2**20
        ),
    )(ensemble, obs_value, obs_var, obs_site, loc_pattern)


def dispatch(nz, nm, ensemble, obs_value, obs_var, obs_site, loc_pattern):
    own = obs_site.shape[1]
    fits = (
        nm == 4 and own * nm == LANES and obs_site.shape[0] == BATCHES and loc_pattern.shape[1:] == (1, 8)
        and ensemble.shape[0] % 16 == 0 and ensemble.shape[1] % (nm * LANES) == 0
    )
    if fits:
        return per_device_kernel(nz, ensemble, obs_value, obs_var, obs_site, loc_pattern)
    return per_device(ensemble, obs_value, obs_var, obs_site, loc_pattern)


def solution(mesh):
    in_specs = (
        P("member", ("groups", "state")),
        P(None, ("groups", "state", "member")),
        P(None, ("groups", "state", "member")),
        P(None, ("groups", "state", "member")),
        P(None, ("groups", "state", "member"), None),
    )
    out_specs = P("member", ("groups", "state"))
    sizes = (mesh.shape["state"], mesh.shape["member"])
    return jax.shard_map(
        functools.partial(dispatch, *sizes), mesh=mesh, in_specs=in_specs, out_specs=out_specs, check_vma=False
    )
```

```python
import functools

import jax
import jax.numpy as jnp
from jax import lax
from jax.experimental import pallas as pl
from jax.experimental.pallas import tpu as pltpu
from jax.sharding import PartitionSpec as P

BATCHES = 6


EPS = 1e-05


def panel_from_prior(prior, ovar, oval):
    members = prior.shape[1]
    ymean = jnp.mean(prior, axis=1, keepdims=True)
    yanom = prior - ymean
    spread = jnp.sum(yanom * yanom, axis=1) / (members - 1.0)
    post_mean = (ymean[:, 0] * ovar + oval * spread) / (ovar + spread)
    shrink = jnp.sqrt(ovar / (ovar + spread))
    incr = (post_mean[:, None] + shrink[:, None] * yanom - prior).astype(jnp.bfloat16)
    gain = 1.0 / ((members - 1.0) * (spread + EPS))
    return (yanom.astype(jnp.bfloat16), incr, gain)


def apply_rows(total, xanom, yanom_b, incr, gain, wrow):
    cov = jnp.dot(yanom_b, xanom, preferred_element_type=jnp.float32)
    weights = (cov * (gain * wrow)[:, None]).astype(jnp.bfloat16)
    return total + lax.dot_general(
        incr, weights, (((0,), (0,)), ((), ())), preferred_element_type=jnp.float32
    )


def per_device(ensemble, obs_value, obs_var, obs_site, loc_pattern):
    gathered = lax.all_to_all(ensemble, "member", split_axis=1, concat_axis=0, tiled=True)
    state = gathered.astype(jnp.float32)
    members = gathered.shape[0]
    own_obs = obs_site.shape[1]
    nblocks = loc_pattern.shape[1] * lax.axis_size(("state", "member"))
    total_obs = own_obs * nblocks
    ntiles = loc_pattern.shape[2]
    obs_tile = total_obs // ntiles
    own_cols = jnp.take(gathered, obs_site.reshape(-1), axis=1)
    all_cols, all_loc = (
        lax.all_gather(own_cols, ("state", "member"), axis=1, tiled=True),
        lax.all_gather(loc_pattern.astype(jnp.bfloat16), ("state", "member"), axis=1, tiled=True),
    )
    all_vals, all_vars = (
        lax.all_gather(obs_value, ("state", "member"), axis=1, tiled=True),
        lax.all_gather(obs_var, ("state", "member"), axis=1, tiled=True),
    )
    columns = all_cols.astype(jnp.float32).reshape(members, nblocks, BATCHES, own_obs)
    columns = columns.transpose(2, 0, 1, 3).reshape(BATCHES, members, total_obs)
    col_block = jnp.arange(total_obs, dtype=jnp.int32) // own_obs
    block_onehot = (col_block[:, None] == jnp.arange(nblocks, dtype=jnp.int32)[None, :]).astype(
        jnp.float32
    )
    obs_tiles = jnp.arange(total_obs, dtype=jnp.int32) // obs_tile
    tile_onehot = (obs_tiles[:, None] == jnp.arange(ntiles, dtype=jnp.int32)[None, :]).astype(
        jnp.float32
    )
    for batch in range(BATCHES):
        prior = columns[batch].T
        yanom_b, incr, gain = panel_from_prior(prior, all_vars[batch], all_vals[batch])
        wrow = jnp.repeat(loc_pattern[batch, 0].astype(jnp.float32), obs_tile)
        xanom = (state - jnp.mean(state, axis=0, keepdims=True)).astype(jnp.bfloat16)
        state = apply_rows(state, xanom, yanom_b, incr, gain, wrow)
        if batch + 1 < BATCHES:
            later = columns[batch + 1 :].transpose(1, 0, 2).reshape(members, -1)
            col_anom = (later - jnp.mean(later, axis=0, keepdims=True)).astype(jnp.bfloat16)
            loc_now = all_loc[batch].astype(jnp.float32)
            col_loc = jnp.dot(
                jnp.dot(block_onehot, loc_now, precision=lax.Precision.HIGHEST),
                tile_onehot.T,
                precision=lax.Precision.HIGHEST,
            )
            wmat = jnp.tile(col_loc.T, (1, BATCHES - batch - 1))
            cov = jnp.dot(yanom_b, col_anom, preferred_element_type=jnp.float32)
            weights = (cov * gain[:, None] * wmat).astype(jnp.bfloat16)
            later = later + lax.dot_general(
                incr, weights, (((0,), (0,)), ((), ())), preferred_element_type=jnp.float32
            )
            later = later.reshape(members, BATCHES - batch - 1, total_obs).transpose(1, 0, 2)
            columns = jnp.concatenate([columns[: batch + 1], later], axis=0)
    return lax.all_to_all(
        state.astype(jnp.bfloat16), "member", split_axis=0, concat_axis=1, tiled=True
    )


LANES = 128
MESH = pl.DeviceIdType.MESH


def row_mean(values):
    return jnp.mean(values, axis=1, keepdims=True)


def ensemble_kernel(
    nz, own, ens_ref, val_ref, var_ref, site_ref, loc_ref, out_ref,
    meta, cols, every, state, ygains, incrs, qstate, vals, lxs, qsend, qrecv,
    val_in, var_in, site_in, loc_in,
    meta_s, meta_r, z_s, z_r, x_s, x_r, c_s, c_r,
    ex_s, ex_r, ec_s, ec_r, ed_s, ed_r, q_s, q_r, local_s,
):
    f32, bf16 = jnp.float32, jnp.bfloat16
    nm = 4
    rows, width = ens_ref.shape
    block = width // nm
    members = rows * nm
    nobs = nz * nm * own
    z, m = lax.axis_index("state"), lax.axis_index("member")

    def peer(dz, dm):
        return {"state": lax.rem(z + dz, nz), "member": jnp.bitwise_xor(m, dm)}

    def send(src, dst, ssem, rsem, dz, dm):
        copy = pltpu.make_async_remote_copy(
            src_ref=src, dst_ref=dst, send_sem=ssem, recv_sem=rsem,
            device_id=peer(dz, dm), device_id_type=MESH,
        )
        copy.start()
        sent.append(copy)
        return copy

    def place(member):
        return pl.multiple_of((member % 2 * 2 + member // 2) * rows, rows)

    base = place(m)
    pair = pl.multiple_of(m % 2 * (2 * rows), 2 * rows)
    pair_c = pl.multiple_of((1 - m % 2) * (2 * rows), 2 * rows)
    base_x = place(jnp.bitwise_xor(m, 2))
    loads = [
        pltpu.make_async_copy(src, dst, local_s.at[at])
        for at, (src, dst) in enumerate((
            (val_ref, val_in), (var_ref, var_in), (site_ref, site_in), (loc_ref, loc_in),
            (ens_ref, every.at[pl.ds(base, rows), :]),
        ))
    ]
    for copy in loads:
        copy.start()

    sent = []
    others = [(dz, dm) for dz in range(nz) for dm in range(nm) if dz or dm]
    barrier = pltpu.get_barrier_semaphore()
    for dz, dm in others:
        pl.semaphore_signal(barrier, inc=1, device_id=peer(dz, dm), device_id_type=MESH)
    for copy in loads[:4]:
        copy.wait()
    mine = z * nm + m
    loc = loc_in[:, 0, :].astype(f32)
    sites = [site_in[b : b + 1, :].astype(f32) for b in range(BATCHES)]
    spare = LANES - 2 * own - loc.shape[1]
    meta[mine, 0:BATCHES, :] = jnp.concatenate(
        [val_in[...], var_in[...], loc, jnp.zeros((BATCHES, spare), f32)], axis=1
    )
    meta[mine, 6:7, :] = jnp.concatenate(sites[:4], axis=1)
    meta[mine, 7:8, :] = jnp.concatenate(
        sites[4:] + [jnp.full((1, LANES - 2 * own), -1.0, f32)], axis=1
    )
    pl.semaphore_wait(barrier, len(others))
    meta_copies = {}
    for dz, dm in others:
        at = dz * nm + dm
        meta_copies[dz, dm] = send(meta.at[mine], meta.at[mine], meta_s.at[at], meta_r.at[at], dz, dm)
    loads[4].wait()
    exc, ecc, edc = {}, {}, {}

    def send_ens(kk):
        there = every.at[pl.ds(base, rows), pl.ds(kk * block, block)]
        exc[kk] = send(there, there, ex_s.at[kk], ex_r.at[kk], 0, 2)
        ecc[kk] = send(there, there, ec_s.at[kk], ec_r.at[kk], 0, 1)

    def relay_ens(kk):
        exc[kk].wait_recv()
        there = every.at[pl.ds(base_x, rows), pl.ds(kk * block, block)]
        edc[kk] = send(there, there, ed_s.at[kk], ed_r.at[kk], 0, 1)

    send_ens(0)
    for dm in range(1, nm):
        meta_copies[0, dm].wait_recv()

    site_iota = lax.broadcasted_iota(jnp.int32, (block, LANES), 0).astype(f32)
    first, second = [], []
    for kk in range(nm):
        got = meta[z * nm + kk]
        piece = every[pl.ds(base, rows), kk * block : (kk + 1) * block]
        for out, r in ((first, 6), (second, 7)):
            onehot = jnp.where(site_iota == got[r : r + 1, :], 1.0, 0.0).astype(bf16)
            out.append(jnp.dot(piece, onehot, preferred_element_type=f32).astype(bf16))
    r_iota = lax.broadcasted_iota(jnp.int32, (nm * LANES, nm * LANES), 0)
    c_iota = lax.broadcasted_iota(jnp.int32, (nm * LANES, nm * LANES), 1)
    target = (r_iota % LANES) // own * LANES + r_iota // LANES * own + r_iota % own
    perm = jnp.where(c_iota == target, 1.0, 0.0).astype(bf16)
    placed = jnp.dot(jnp.concatenate(first, axis=1), perm, preferred_element_type=f32).astype(bf16)
    placed2 = jnp.dot(
        jnp.concatenate(second, axis=1), perm[:, : 2 * LANES], preferred_element_type=f32
    ).astype(bf16)
    cols[z, pl.ds(base, rows), 0 : nm * LANES] = placed
    cols[z, pl.ds(base, rows), nm * LANES : BATCHES * LANES] = placed2

    chunks = ((0, 1), (1, 3), (3, 4), (4, BATCHES))

    def view(d, c, start, count):
        low, high = chunks[c]
        lanes = pl.ds(low * LANES, (high - low) * LANES)
        return cols.at[lax.rem(z - d + nz, nz), pl.ds(start, count), lanes]

    zc, xc, cc = {}, {}, {}

    def go_z(c, start, count):
        v = view(0, c, start, count)
        for d in range(1, nz):
            at = c * nz + d
            zc[c, d] = send(v, v, z_s.at[at], z_r.at[at], d, 0)

    def go_x(c, d):
        at, v = c * nz + d, view(d, c, base, rows)
        xc[c, d] = send(v, v, x_s.at[at], x_r.at[at], 0, 2)

    def go_core(c, d):
        at, v = c * nz + d, view(d, c, pair, 2 * rows)
        cc[c, d] = send(v, v, c_s.at[at], c_r.at[at], 0, 1)

    def arrive(c):
        for d in range(nz):
            cc[c, d].wait_recv()

    go_x(0, 0)
    go_x(2, 0)
    go_x(3, 0)
    go_x(1, 0)
    xc[0, 0].wait_recv()
    go_z(0, pair, 2 * rows)
    go_core(0, 0)
    go_z(1, base, rows)

    for dz, dm in others:
        if dz:
            meta_copies[dz, dm].wait_recv()
    for k in range(nz * nm):
        turned = meta[k].T
        vals[0, k * own : (k + 1) * own, :] = turned[0:own, :]
        vals[1, k * own : (k + 1) * own, :] = turned[own : 2 * own, :]
    ntiles = 8
    er = lax.broadcasted_iota(jnp.int32, (LANES, nobs), 0)
    ec = lax.broadcasted_iota(jnp.int32, (LANES, nobs), 1)
    expand = jnp.where(er == ec // (nobs // ntiles) + 2 * own, 1.0, 0.0).astype(bf16)
    own_loc = jnp.dot(meta[mine].astype(bf16), expand, preferred_element_type=f32)
    wide = jnp.dot(
        meta[...].reshape(nz * nm * 8, LANES).astype(bf16), expand, preferred_element_type=f32
    ).reshape(nz * nm, 8, nobs)
    for b in range(BATCHES):
        lxs[b] = wide[:, b, :]

    for d in range(1, nz):
        zc[0, d].wait_recv()
        go_core(0, d)
    for d in range(1, nz):
        zc[1, d].wait_recv()
        go_x(1, d)
    for c in (2, 3):
        xc[c, 0].wait_recv()
        go_z(c, pair, 2 * rows)
        go_core(c, 0)
    for kk in range(1, nm):
        send_ens(kk)

    def unpack(b):
        for zz in range(nz):
            got = cols[zz, :, b * LANES : (b + 1) * LANES].astype(f32)
            state[b, zz * LANES : (zz + 1) * LANES, :] = got.T

    qr = lax.broadcasted_iota(jnp.int32, (members, members), 0)
    qc = lax.broadcasted_iota(jnp.int32, (members, members), 1)
    eye = jnp.where(qr == qc, 1.0, 0.0)
    contract = (((1,), (1,)), ((), ()))

    for b in range(BATCHES):
        for c, (low, high) in enumerate(chunks):
            if b == low:
                if c == 1:
                    for d in range(nz):
                        xc[1, d].wait_recv()
                        go_core(1, d)
                if c >= 2:
                    for d in range(1, nz):
                        zc[c, d].wait_recv()
                        go_core(c, d)
                if c == 2:
                    relay_ens(0)
                arrive(c)
                for fresh in range(low, high):
                    unpack(fresh)

        if b:
            @pl.loop(0, b)
            def _(earlier):
                x = state[b]
                xanom = (x - row_mean(x)).astype(bf16)
                cov = lax.dot_general(xanom, ygains[earlier], contract, preferred_element_type=f32)
                cov = cov.reshape(nz * nm, own, nobs) * lxs[earlier][:, None, :]
                weights = cov.reshape(nobs, nobs).astype(bf16)
                state[b] = x + jnp.dot(weights, incrs[earlier], preferred_element_type=f32)

        prior = state[b]
        ovar, oval = vals[1, :, b : b + 1], vals[0, :, b : b + 1]
        ymean = row_mean(prior)
        yanom = prior - ymean
        spread = jnp.sum(yanom * yanom, axis=1, keepdims=True) / (members - 1.0)
        post_mean = (ymean * ovar + oval * spread) / (ovar + spread)
        shrink = jnp.sqrt(ovar / (ovar + spread))
        incr = (post_mean + shrink * yanom - prior).astype(bf16)
        gain = 1.0 / ((members - 1.0) * (spread + EPS))
        ygain = (yanom * gain).astype(bf16)
        if b + 1 < BATCHES:
            ygains[b] = ygain
            incrs[b] = incr

        if b == 0:
            weights = (lax.dot_general(eye.astype(bf16), ygain, contract, preferred_element_type=f32)
                       * own_loc[0:1, :]).astype(bf16)
            qstate[...] = jnp.dot(weights, incr, preferred_element_type=f32)
        else:
            q = qstate[...]
            xanom = (q - row_mean(q) + eye).astype(bf16)
            weights = (lax.dot_general(xanom, ygain, contract, preferred_element_type=f32)
                       * own_loc[b : b + 1, :]).astype(bf16)
            qstate[...] = q + jnp.dot(weights, incr, preferred_element_type=f32)
        if b >= 4:
            relay_ens(b - 3)

    q = qstate[...]
    q = (q - jnp.mean(q, axis=0, keepdims=True)).T.astype(bf16)
    qsend[...] = q
    qrecv[m] = qsend[pl.ds(base, rows), :]
    qcs = []
    for dm in range(1, nm):
        to = place(jnp.bitwise_xor(m, dm))
        qcs.append(send(qsend.at[pl.ds(to, rows), :], qrecv.at[m], q_s.at[dm], q_r.at[dm], 0, dm))
    relay_ens(nm - 1)
    for copy in qcs:
        copy.wait_recv()
    for kk in range(nm):
        ecc[kk].wait_recv()
        edc[kk].wait_recv()
        part = slice(kk * block, (kk + 1) * block)
        delta = jnp.dot(qrecv[kk], every[:, part], preferred_element_type=f32)
        out_ref[:, part] = (every[pl.ds(base, rows), part].astype(f32) + delta).astype(bf16)
    for copy in sent:
        copy.wait_send()


def per_device_kernel(nz, ensemble, obs_value, obs_var, obs_site, loc_pattern):
    nm = 4
    own = obs_site.shape[1]
    rows, width = ensemble.shape
    members, nobs, block = rows * nm, nz * nm * own, width // nm
    dma, bf16, f32 = pltpu.SemaphoreType.DMA, jnp.bfloat16, jnp.float32
    two = [dma((4 * nz,))] * 2
    return pl.pallas_call(
        functools.partial(ensemble_kernel, nz, own),
        out_shape=jax.ShapeDtypeStruct(ensemble.shape, bf16),
        in_specs=[pl.BlockSpec(memory_space=pl.ANY)] * 5,
        out_specs=pl.BlockSpec(memory_space=pltpu.VMEM),
        scratch_shapes=[
            pltpu.VMEM((nz * nm, 8, LANES), f32),
            pltpu.VMEM((nz, members, BATCHES * LANES), bf16),
            pltpu.VMEM((members, width), bf16),
            pltpu.VMEM((BATCHES, nobs, members), f32),
            pltpu.VMEM((BATCHES - 1, nobs, members), bf16),
            pltpu.VMEM((BATCHES - 1, nobs, members), bf16),
            pltpu.VMEM((members, members), f32),
            pltpu.VMEM((2, nobs, 8), f32),
            pltpu.VMEM((BATCHES, nz * nm, nobs), f32),
            pltpu.VMEM((members, members), bf16),
            pltpu.VMEM((nm, rows, members), bf16),
            pltpu.VMEM(obs_value.shape, f32),
            pltpu.VMEM(obs_var.shape, f32),
            pltpu.VMEM(obs_site.shape, jnp.int32),
            pltpu.VMEM(loc_pattern.shape, jnp.int32),
            dma((nz * nm,)), dma((nz * nm,)),
            *two, *two, *two,
            *[dma((nm,))] * 8,
            dma((5,)),
        ],
        compiler_params=pltpu.CompilerParams(
            collective_id=0, has_side_effects=True, vmem_limit_bytes=56 * 2**20
        ),
    )(ensemble, obs_value, obs_var, obs_site, loc_pattern)


def dispatch(nz, nm, ensemble, obs_value, obs_var, obs_site, loc_pattern):
    own = obs_site.shape[1]
    fits = (
        nm == 4 and own * nm == LANES and obs_site.shape[0] == BATCHES and loc_pattern.shape[1:] == (1, 8)
        and ensemble.shape[0] % 16 == 0 and ensemble.shape[1] % (nm * LANES) == 0
    )
    if fits:
        return per_device_kernel(nz, ensemble, obs_value, obs_var, obs_site, loc_pattern)
    return per_device(ensemble, obs_value, obs_var, obs_site, loc_pattern)


def solution(mesh):
    in_specs = (
        P("member", ("groups", "state")),
        P(None, ("groups", "state", "member")),
        P(None, ("groups", "state", "member")),
        P(None, ("groups", "state", "member")),
        P(None, ("groups", "state", "member"), None),
    )
    out_specs = P("member", ("groups", "state"))
    sizes = (mesh.shape["state"], mesh.shape["member"])
    return jax.shard_map(
        functools.partial(dispatch, *sizes), mesh=mesh, in_specs=in_specs, out_specs=out_specs, check_vma=False
    )
```
